256 devices in a mesh: ctx: 32 (over y, z), grp: 8 (over x, core).
Axes of the slice: x: 4, y: 4, z: 8, core: 2. Of those that a mesh axis runs over, the one named last changes fastest.
Arguments:
- streams: bfloat16 [3, 12288, 4096], P(None, 'ctx', 'grp'), may hold values from -400 to 400
- filters: bfloat16 [3, 256, 128], P(None, 'grp'), may hold values from -0.5 to 0.5
- gain: float32 [4096], P('grp'), may hold values from 0.5 to 1.5
Outputs:
- normed: bfloat16 [12288, 4096], P('ctx', 'grp')
The draws below stay inside these ranges and needn't reach their ends.
All inputs are finite; a program needn't handle non-finite values.
Results may differ from the reference program's by a relative error of at most 0.012.
The reference program's roundings to bfloat16 on the way count: a program that leaves them out, or rounds other values in their place, can miss the bound.
Values may be sent and summed in bfloat16 or wider, within the bound.
No kernel may reach another device: no remote copies, remote signals or barrier semaphores. Data moves between devices by JAX's collectives and lax.ppermute only.
A program may use at most 128 MiB of HBM per device.

```python
import math
import jax
import jax.numpy as jnp
import numpy as np
from jax import lax

HEADS = 32
HD = 128
FG = 256
FLEN = 128
CH = 4096
LEN = 12288


def draw_streams(key, part):
    key_list = jax.random.split(key, 2)
    base = jnp.clip(jax.random.normal(key_list[0], (3, LEN, CH), jnp.float32), -4.0, 4.0)
    chan_top = 10.0
    chan_scale = jnp.exp(math.log(chan_top) * jnp.arange(CH, dtype=jnp.float32) / (CH - 1))
    tok_scale = jnp.exp(jax.random.uniform(key_list[1], (LEN,), jnp.float32, 0.0, math.log(3.0)))
    base = base.at[2].multiply(tok_scale[:, None] * chan_scale[None, :])
    return base.astype(jnp.bfloat16)


def level_of(own_key, extent, shards, least, largest):
    factor_of = 1.0
    for dim, shards_of in shards:
        draws = jax.random.uniform(jax.random.fold_in(jax.random.fold_in(own_key, 6), dim), (shards_of,), jnp.float32, least / len(shards), largest / len(shards))
        factor_of = factor_of * jnp.repeat(jnp.exp(draws), extent[dim] // shards_of).reshape((-1,) + (1,) * (len(extent) - 1 - dim))
    return factor_of


def scatter_about(stream_key, extent, width, most, shards=(), kind=jnp.bfloat16):
    level = level_of(stream_key, extent, shards, -0.22, 0.18) if shards else 1.0
    values = jax.random.normal(stream_key, extent, jnp.float32) * width * level
    return jnp.minimum(jnp.maximum(values, -most), most).astype(kind)


def setup_inputs(seed: int = 0) -> dict:
    key_of = jax.random.split(jax.random.key(seed), 4)
    return {
        "streams": draw_streams(jax.random.fold_in(key_of[3], 71), 0),
        "filters": scatter_about(key_of[1], (3, FG, FLEN), FLEN ** -0.5, 0.5, ((1, 8),)),
        "gain": jnp.clip(1.0 + 0.1 * jax.random.normal(key_of[2], (CH,), jnp.float32), 0.5, 1.5),
    }


def filter_stream(values, taps):
    group_width = CH // FG
    block_count = LEN // FLEN
    lag_table = np.arange(FLEN)[:, None] - np.arange(FLEN)[None, :]
    lower_idx = np.where(lag_table >= 0, lag_table, 0)
    upper_idx = np.where(lag_table < 0, lag_table + FLEN, 0)
    taps_wide = taps.astype(jnp.float32)
    lower = jnp.where(lag_table >= 0, taps_wide[:, lower_idx], 0.0)
    upper = jnp.where(lag_table < 0, taps_wide[:, upper_idx], 0.0)
    wide = values.astype(jnp.float32)
    padded = jnp.concatenate([jnp.zeros((FLEN, CH), wide.dtype), wide], axis=0)
    blocks = padded.reshape(block_count + 1, FLEN, FG, group_width)
    result = jnp.einsum('gts,bsgc->btgc', lower, blocks[1:], precision=lax.Precision.HIGHEST)
    result = result + jnp.einsum('gts,bsgc->btgc', upper, blocks[:-1], precision=lax.Precision.HIGHEST)
    return result.reshape(LEN, CH).astype(jnp.bfloat16)

def reference(streams, filters, gain):
    features = [filter_stream(streams[idx], filters[idx]) for idx in range(3)]
    split = [feat.reshape(LEN, HEADS, HD).transpose(1, 0, 2) for feat in features]
    block_rows = math.gcd(LEN, 1024)
    outputs = []
    for block_idx in range(LEN // block_rows):
        first = block_idx * block_rows
        key_len = first + block_rows
        query_pos = first + jnp.arange(block_rows, dtype=jnp.int32)
        key_pos = jnp.arange(key_len, dtype=jnp.int32)
        causal = query_pos[:, None] >= key_pos[None, :]

        def head_attention(triple):
            query, keyed, valued = triple
            scores = jnp.dot(query, keyed.T, preferred_element_type=jnp.float32) * HD ** (-0.5)
            top = lax.optimization_barrier(jnp.max(jnp.where(causal, scores, -1e+30), axis=1))
            weights = jnp.where(causal, jnp.exp(scores - top[:, None]), 0.0)
            numer = jnp.dot(weights.astype(jnp.bfloat16), valued, preferred_element_type=jnp.float32)
            return (numer / lax.optimization_barrier(jnp.sum(weights, axis=1))[:, None]).astype(jnp.bfloat16)
        per_head = lax.map(head_attention, (split[0][:, first:key_len], split[1][:, :key_len], split[2][:, :key_len]))
        outputs.append(per_head.transpose(1, 0, 2).reshape(block_rows, CH))
    attended = jnp.concatenate(outputs, axis=0)
    wide = attended.astype(jnp.float32)
    power = lax.optimization_barrier(jnp.mean(wide * wide, axis=1))
    return (wide * gain[None, :] / jnp.sqrt(power + 1e-06)[:, None]).astype(jnp.bfloat16)
```

```python
import functools
import math

import jax
import jax.numpy as jnp
from jax import lax
from jax.experimental import pallas as pl
from jax.experimental.pallas import tpu as pltpu
from jax.sharding import Mesh
from jax.sharding import PartitionSpec as P

HD = 128
CH = 4096
NY, NZ, NX, NC = 4, 8, 4, 2
AXES = ("y", "z", "x", "c")
TOK = 384
TAP = 128
GW = 16
GH = HD // GW
ROWS = 4 * TOK
EXP2_SCALE = math.log2(math.e) / math.sqrt(HD)
FULL = pl.BlockSpec(memory_space=pltpu.VMEM)
LIMIT = 48 * 2**20


def linear(y, z, x, c):
    return ((y * NZ + z) * NX + x) * NC + c


def coords():
    for y in range(NY):
        for z in range(NZ):
            for x in range(NX):
                for c in range(NC):
                    yield y, z, x, c


def route(move):
    pairs = []
    for at in coords():
        to = move(*at)
        if to is not None:
            pairs.append((linear(*at), linear(*to)))
    return pairs


def send(block, move):
    return lax.ppermute(block, AXES, route(move))


def to_owner(step):
    def move(y, z, x, c):
        r = z if y % 2 == 0 else 7 - z
        return r // 2, 4 * c + (y + step) % 4, x, r % 2

    return move


def send_home(block, step):
    pairs = [(b, a) for a, b in route(to_owner(step))]
    return lax.ppermute(block, AXES, pairs)


def swap_core(y, z, x, c):
    return y, z, x, 1 - c


def shift_y(by):
    return lambda y, z, x, c: ((y + by) % NY, z, x, c)


def shift_x(by):
    return lambda y, z, x, c: (y, z, (x + by) % NX, c)


def shift_owner(by):
    def move(y, z, x, c):
        r = 2 * y + c + by
        return (r // 2, z, x, r % 2) if 0 <= r < 8 else None

    return move


def dot_nt(a, b):
    return lax.dot_general(a, b, (((1,), (1,)), ((), ())), preferred_element_type=jnp.float32)


def table_kernel(first_row, q_table, kv_table):
    for s in range(3):
        for g in range(GH):
            i = s * GH + g
            row = jnp.broadcast_to(first_row[i : i + 1, :], (TAP, 2 * TAP))
            band = pltpu.roll(row, 0, 1, stride=1, stride_axis=0).astype(jnp.bfloat16)
            if s == 0:
                q_table[0, g * TAP : (g + 1) * TAP, :] = band
            else:
                kv_table[s - 1, g * TAP : (g + 1) * TAP, :] = band


def make_tables(first_row):
    return pl.pallas_call(
        table_kernel,
        out_shape=[
            jax.ShapeDtypeStruct((1, GH * TAP, 2 * TAP), jnp.bfloat16),
            jax.ShapeDtypeStruct((2, GH * TAP, 2 * TAP), jnp.bfloat16),
        ],
        in_specs=[FULL],
        out_specs=[FULL, FULL],
        compiler_params=pltpu.CompilerParams(vmem_limit_bytes=LIMIT),
        name="tables",
    )(first_row)


def filter_kernel(n, at, table, p0, p1, p2, p3, up, down, out):
    pieces = (p0, p1, p2, p3)
    r = at[0]
    z = at[1]
    lane_group = lax.broadcasted_iota(jnp.int32, (TAP, HD), 1) // GW
    for k in range(4):
        slot = lax.rem(z - k + 8, 4)
        own = jnp.logical_or(
            jnp.logical_and(slot == 2, r == 0), jnp.logical_and(lax.rem(slot, 2) == 1, r == 7)
        )
        from_up = lax.rem(slot, 2) == 0
        for s in range(n):
            before = jnp.where(
                own,
                pieces[(k + 1) % 4][s, TOK - TAP :, :],
                jnp.where(from_up, up[k, s], down[k, s]),
            )
            for t in range(TOK // TAP):
                now = pieces[k][s, t * TAP : (t + 1) * TAP, :]
                both = jnp.concatenate([before, now], axis=0)
                wide = jnp.dot(table[s], both, preferred_element_type=jnp.float32)
                res = wide[0:TAP]
                for g in range(1, GH):
                    res = jnp.where(lane_group == g, wide[g * TAP : (g + 1) * TAP], res)
                start = pl.multiple_of(slot * TOK + t * TAP, TAP)
                out[s, pl.ds(start, TAP), :] = res.astype(jnp.bfloat16)
                before = now


def filter_pieces(at, table, pieces, up, down):
    n = table.shape[0]
    return pl.pallas_call(
        functools.partial(filter_kernel, n),
        out_shape=jax.ShapeDtypeStruct((n, ROWS, HD), jnp.bfloat16),
        in_specs=[pl.BlockSpec(memory_space=pltpu.SMEM)] + [FULL] * 7,
        out_specs=FULL,
        compiler_params=pltpu.CompilerParams(vmem_limit_bytes=LIMIT),
        name="filter%d" % n,
    )(at, table, *pieces, up, down)


def attend_unit(q, parts, state, slot, length, first=False, diag=False):
    acc, top, total = state
    rows = slice(slot * TOK, (slot + 1) * TOK)
    used = []
    left = length
    for ref, size in parts:
        if left > 0:
            used.append((ref, min(left, size)))
            left -= size
    cols = []
    for ref, size in used:
        scores = dot_nt(q[rows, :], ref[0, 0:size, :])
        cols += [scores[:, j * 128 : (j + 1) * 128] for j in range(size // 128)]
    if diag:
        row = lax.broadcasted_iota(jnp.int32, (TOK, 128), 0)
        col = lax.broadcasted_iota(jnp.int32, (TOK, 128), 1)
        for d in range(TOK // 128):
            j = len(cols) - TOK // 128 + d
            cols[j] = jnp.where(col + d * 128 <= row, cols[j], -1e30)
    high = functools.reduce(jnp.maximum, cols)
    high = jnp.broadcast_to(jnp.max(high, axis=1, keepdims=True), (TOK, 128))
    if not first:
        old = top[rows, :]
        high = jnp.maximum(old, high)
        fade = jnp.exp2((old - high) * EXP2_SCALE)
    weights = [jnp.exp2((s - high) * EXP2_SCALE) for s in cols]
    added = functools.reduce(jnp.add, weights)
    rounded = jnp.concatenate([w.astype(jnp.bfloat16) for w in weights], axis=1)
    res = None
    done = 0
    for ref, size in used:
        part = jnp.dot(
            rounded[:, done : done + size], ref[1, 0:size, :], preferred_element_type=jnp.float32
        )
        res = part if res is None else res + part
        done += size
    top[rows, :] = high
    if first:
        total[rows, :] = added
        acc[rows, :] = res
    else:
        total[rows, :] = total[rows, :] * fade + added
        acc[rows, :] = acc[rows, :] * fade + res


def attend_chunk(q, parts, state, earlier):
    @pl.when(earlier)
    def _():
        for slot, blocks in enumerate((1, 1, 3, 3)):
            attend_unit(q, parts, state, slot, blocks * TOK)

    @pl.when(jnp.logical_not(earlier))
    def _():
        for slot, blocks in enumerate((0, 2, 2, 4)):
            if blocks:
                attend_unit(q, parts, state, slot, blocks * TOK)


def begin_kernel(at, q, own, partner, acc, top, total):
    state = (acc, top, total)
    q = q.at[0]
    for slot in range(4):
        attend_unit(q, [(own, ROWS)], state, slot, (slot + 1) * TOK, first=True, diag=True)
    attend_chunk(q, [(partner, ROWS)], state, lax.rem(at[0], 2) == 1)


def middle_kernel(at, q, below, above, acc_in, top_in, total_in, acc, top, total):
    acc[...] = acc_in[...]
    top[...] = top_in[...]
    total[...] = total_in[...]
    state = (acc, top, total)
    q = q.at[0]
    y = at[0] // 2
    attend_chunk(q, [(below, ROWS)], state, y > 0)
    attend_chunk(q, [(above, ROWS)], state, y == 3)


def end_kernel(at, q, fa, fb, sa, sb, acc_in, top_in, total_in, o0, o1, o2, o3, acc, top, total):
    acc[...] = acc_in[...]
    top[...] = top_in[...]
    total[...] = total_in[...]
    state = (acc, top, total)
    q = q.at[0]
    earlier = at[0] >= 4
    half = ROWS // 2
    attend_chunk(q, [(fa, half), (fb, half)], state, earlier)
    attend_chunk(q, [(sa, half), (sb, half)], state, earlier)
    for k, out in enumerate((o0, o1, o2, o3)):
        rows = pl.ds(pl.multiple_of(lax.rem(at[1] - k + 8, 4) * TOK, TAP), TOK)
        whole = jnp.sum(total[rows, :], axis=1, keepdims=True)
        out[...] = (acc[rows, :] / whole).astype(jnp.bfloat16)


STATE = [jax.ShapeDtypeStruct((ROWS, HD), jnp.float32)] * 3
UNIT_FLOPS = 4 * TOK * TOK * HD


def attend_call(kernel, name, units, outs, scratch, args):
    return pl.pallas_call(
        kernel,
        out_shape=outs,
        in_specs=[pl.BlockSpec(memory_space=pltpu.SMEM)] + [FULL] * (len(args) - 1),
        out_specs=[FULL] * len(outs),
        scratch_shapes=scratch,
        compiler_params=pltpu.CompilerParams(vmem_limit_bytes=LIMIT),
        cost_estimate=pl.CostEstimate(
            flops=2 * units * UNIT_FLOPS,
            bytes_accessed=6 * 2**20,
            transcendentals=units * TOK * TOK,
        ),
        name=name,
    )(*args)


def squares_kernel(p0, p1, p2, p3, out):
    wide = sum(jnp.square(p[...].astype(jnp.float32)) for p in (p0, p1, p2, p3))
    out[...] = jnp.sum(wide.T, axis=0, keepdims=True)


def norm_kernel(at, p0, p1, p2, p3, s0, s1, s2, s3, gain, out):
    power = (s0[...] + s1[...] + s2[...] + s3[...]) * (1.0 / CH)
    scale = jnp.broadcast_to(lax.rsqrt(power + 1e-6), (HD, TOK)).T
    for k, piece in enumerate((p0, p1, p2, p3)):
        cols = pl.ds(pl.multiple_of(lax.rem(at[2] + k, 4) * HD, HD), HD)
        out[:, cols] = (piece[...].astype(jnp.float32) * gain[:, cols] * scale).astype(jnp.bfloat16)


def local(streams, filters, gain):
    y, z, c = lax.axis_index("y"), lax.axis_index("z"), lax.axis_index("c")
    at = jnp.stack([2 * y + c, z, y, c]).astype(jnp.int32)

    kv, q = [], []
    for k in range(4):
        col = lax.rem(y + k, 4) * HD
        kv.append(send(lax.dynamic_slice(streams, (1, 0, col), (2, TOK, HD)), to_owner(k)))
    for k in range(4):
        col = lax.rem(y + k, 4) * HD
        q.append(send(lax.dynamic_slice(streams, (0, 0, col), (1, TOK, HD)), to_owner(k)))

    mine = lax.dynamic_slice(filters, (0, lax.rem(z, 4) * GH, 0), (3, GH, TAP))
    other = send(mine, swap_core)
    taps = jnp.where(c == z // 4, mine, other).reshape(3 * GH, TAP).astype(jnp.float32)
    q_table, kv_table = make_tables(jnp.pad(taps[:, ::-1], ((0, 0), (1, TAP - 1))))

    def filtered(pieces, table):
        tails = jnp.stack([p[:, TOK - TAP :, :] for p in pieces])
        up = send(tails, shift_owner(1))
        down = send(tails, shift_owner(-1))
        return filter_pieces(at, table, pieces, up, down)

    own = filtered(kv, kv_table)
    from_below = send(own, shift_y(1))
    from_above = send(own, shift_y(-1))
    partner = send(own, swap_core)
    queries = filtered(q, q_table)

    state = attend_call(
        begin_kernel, "attend_begin", 18, STATE, [], (at, queries, own, partner)
    )
    half = ROWS // 2
    far_a = send(from_below[:, :half], shift_y(1))
    far_b = send(from_above[:, half:], shift_y(-1))
    swapped_below = send(from_below, swap_core)
    swapped_above = send(from_above, swap_core)
    state = attend_call(
        middle_kernel, "attend_near", 16, STATE, [], (at, queries, from_below, from_above, *state)
    )
    state = attend_call(
        middle_kernel,
        "attend_swapped",
        16,
        STATE,
        [],
        (at, queries, swapped_below, swapped_above, *state),
    )
    swapped_a = send(far_a, swap_core)
    swapped_b = send(far_b, swap_core)
    pieces = attend_call(
        end_kernel,
        "attend_far",
        16,
        [jax.ShapeDtypeStruct((TOK, HD), jnp.bfloat16)] * 4,
        [pltpu.VMEM((ROWS, HD), jnp.float32)] * 3,
        (at, queries, far_a, far_b, swapped_a, swapped_b, *state),
    )

    home = [send_home(p, k) for k, p in enumerate(pieces)]
    part = pl.pallas_call(
        squares_kernel,
        out_shape=jax.ShapeDtypeStruct((1, TOK), jnp.float32),
        in_specs=[FULL] * 4,
        out_specs=FULL,
        name="squares",
    )(*home)
    part = part + send(part, swap_core)
    sums = [part] + [send(part, shift_x(i)) for i in (1, 2, 3)]
    return pl.pallas_call(
        norm_kernel,
        out_shape=jax.ShapeDtypeStruct((TOK, 4 * HD), jnp.bfloat16),
        in_specs=[pl.BlockSpec(memory_space=pltpu.SMEM)] + [FULL] * 9,
        out_specs=FULL,
        name="norm",
    )(at, *home, *sums, gain.reshape(1, 4 * HD))


def solution(mesh):
    split = Mesh(mesh.devices.reshape(NY, NZ, NX, NC), AXES)
    ctx, grp = ("y", "z"), ("x", "c")
    return jax.shard_map(
        local,
        mesh=split,
        in_specs=(P(None, ctx, grp), P(None, grp, None), P(grp)),
        out_specs=P(ctx, grp),
        check_vma=False,
    )
```

```python
import functools
import math

import jax
import jax.numpy as jnp
from jax import lax
from jax.experimental import pallas as pl
from jax.experimental.pallas import tpu as pltpu
from jax.sharding import Mesh
from jax.sharding import PartitionSpec as P

HD = 128
CH = 4096
NY, NZ, NX, NC = 4, 8, 4, 2
AXES = ("y", "z", "x", "c")
TOK = 384
TAP = 128
GW = 16
GH = HD // GW
ROWS = 4 * TOK
EXP2_SCALE = math.log2(math.e) / math.sqrt(HD)
FULL = pl.BlockSpec(memory_space=pltpu.VMEM)
LIMIT = 48 * 2**20


def linear(y, z, x, c):
    return ((y * NZ + z) * NX + x) * NC + c


def coords():
    for y in range(NY):
        for z in range(NZ):
            for x in range(NX):
                for c in range(NC):
                    yield y, z, x, c


def route(move):
    pairs = []
    for at in coords():
        to = move(*at)
        if to is not None:
            pairs.append((linear(*at), linear(*to)))
    return pairs


def send(block, move):
    return lax.ppermute(block, AXES, route(move))


def to_owner(step):
    def move(y, z, x, c):
        r = z if y % 2 == 0 else 7 - z
        return r // 2, 4 * c + (y + r + step) % 4, x, r % 2

    return move


def send_home(block, step):
    pairs = [(b, a) for a, b in route(to_owner(step))]
    return lax.ppermute(block, AXES, pairs)


def swap_core(y, z, x, c):
    return y, z, x, 1 - c


def shift_y(by):
    return lambda y, z, x, c: ((y + by) % NY, z, x, c)


def shift_x(by):
    return lambda y, z, x, c: (y, z, (x + by) % NX, c)


def shift_owner(by):
    def move(y, z, x, c):
        r = 2 * y + c + by
        return (r // 2, z, x, r % 2) if 0 <= r < 8 else None

    return move


def dot_nt(a, b):
    return lax.dot_general(a, b, (((1,), (1,)), ((), ())), preferred_element_type=jnp.float32)


def table_kernel(first_row, table):
    for i in range(3 * GH):
        row = jnp.broadcast_to(first_row[i : i + 1, :], (TAP, 2 * TAP))
        band = pltpu.roll(row, 0, 1, stride=1, stride_axis=0)
        table[i // GH, (i % GH) * TAP : (i % GH + 1) * TAP, :] = band.astype(jnp.bfloat16)


def make_tables(first_row):
    return pl.pallas_call(
        table_kernel,
        out_shape=jax.ShapeDtypeStruct((3, GH * TAP, 2 * TAP), jnp.bfloat16),
        in_specs=[FULL],
        out_specs=FULL,
        compiler_params=pltpu.CompilerParams(vmem_limit_bytes=LIMIT),
        name="tables",
    )(first_row)


def slot_of(at, k):
    return lax.rem(at[1] - at[0] - k + 16, 4)


def filter_kernel(at, table, p0, p1, p2, p3, up, down, q_out, kv_out):
    pieces = (p0, p1, p2, p3)
    r = at[0]
    lane_group = lax.broadcasted_iota(jnp.int32, (TAP, HD), 1) // GW
    slots = [slot_of(at, k) for k in range(4)]
    for s in range(3):
        out = q_out.at[0] if s == 0 else kv_out.at[s - 1]
        tiles = []
        for k, slot in enumerate(slots):
            own = jnp.logical_or(
                jnp.logical_and(slot == 2, r == 0),
                jnp.logical_and(lax.rem(slot, 2) == 1, r == 7),
            )
            before = jnp.where(
                own,
                pieces[(k + 1) % 4][s, TOK - TAP :, :],
                jnp.where(lax.rem(slot, 2) == 0, up[(k + 1) % 4, s], down[(k + 3) % 4, s]),
            )
            for t in range(TOK // TAP):
                now = pieces[k][s, t * TAP : (t + 1) * TAP, :]
                start = pl.multiple_of(slot * TOK + t * TAP, TAP)
                tiles.append((start, jnp.concatenate([before, now], axis=0)))
                before = now
        for i in range(0, len(tiles), 2):
            pair = jnp.concatenate([tiles[i][1], tiles[i + 1][1]], axis=1)
            wide = jnp.dot(table[s], pair, preferred_element_type=jnp.float32)
            for h in range(2):
                cols = slice(h * HD, (h + 1) * HD)
                res = wide[0:TAP, cols]
                for g in range(1, GH):
                    res = jnp.where(lane_group == g, wide[g * TAP : (g + 1) * TAP, cols], res)
                out[pl.ds(tiles[i + h][0], TAP), :] = res.astype(jnp.bfloat16)


def filter_pieces(at, table, pieces, up, down):
    return pl.pallas_call(
        filter_kernel,
        out_shape=[
            jax.ShapeDtypeStruct((1, ROWS, HD), jnp.bfloat16),
            jax.ShapeDtypeStruct((2, ROWS, HD), jnp.bfloat16),
        ],
        in_specs=[pl.BlockSpec(memory_space=pltpu.SMEM)] + [FULL] * 7,
        out_specs=[FULL] * 2,
        compiler_params=pltpu.CompilerParams(vmem_limit_bytes=LIMIT),
        name="filter",
    )(at, table, *pieces, up, down)


def attend_unit(q, parts, state, slot, length, first=False, diag=False):
    acc, top, total = state
    rows = slice(slot * TOK, (slot + 1) * TOK)
    used = []
    left = length
    for ref, size in parts:
        if left > 0:
            used.append((ref, min(left, size)))
            left -= size
    cols = []
    for ref, size in used:
        scores = dot_nt(q[rows, :], ref[0, 0:size, :])
        cols += [scores[:, j * 128 : (j + 1) * 128] for j in range(size // 128)]
    if diag:
        row = lax.broadcasted_iota(jnp.int32, (TOK, 128), 0)
        col = lax.broadcasted_iota(jnp.int32, (TOK, 128), 1)
        for d in range(TOK // 128):
            j = len(cols) - TOK // 128 + d
            cols[j] = jnp.where(col + d * 128 <= row, cols[j], -1e30)
    high = functools.reduce(jnp.maximum, cols)
    high = jnp.broadcast_to(jnp.max(high, axis=1, keepdims=True), (TOK, 128))
    if not first:
        old = top[rows, :]
        high = jnp.maximum(old, high)
        fade = jnp.exp2((old - high) * EXP2_SCALE)
    weights = [jnp.exp2((s - high) * EXP2_SCALE) for s in cols]
    added = functools.reduce(jnp.add, weights)
    rounded = jnp.concatenate([w.astype(jnp.bfloat16) for w in weights], axis=1)
    res = None
    done = 0
    for ref, size in used:
        part = jnp.dot(
            rounded[:, done : done + size], ref[1, 0:size, :], preferred_element_type=jnp.float32
        )
        res = part if res is None else res + part
        done += size
    top[rows, :] = high
    if first:
        total[rows, :] = added
        acc[rows, :] = res
    else:
        total[rows, :] = total[rows, :] * fade + added
        acc[rows, :] = acc[rows, :] * fade + res


def attend_chunk(q, parts, state, earlier):
    @pl.when(earlier)
    def _():
        for slot, blocks in enumerate((1, 1, 3, 3)):
            attend_unit(q, parts, state, slot, blocks * TOK)

    @pl.when(jnp.logical_not(earlier))
    def _():
        for slot, blocks in enumerate((0, 2, 2, 4)):
            if blocks:
                attend_unit(q, parts, state, slot, blocks * TOK)


def begin_kernel(at, q, own, partner, acc, top, total):
    state = (acc, top, total)
    q = q.at[0]
    for slot in range(4):
        attend_unit(q, [(own, ROWS)], state, slot, (slot + 1) * TOK, first=True, diag=True)
    attend_chunk(q, [(partner, ROWS)], state, lax.rem(at[0], 2) == 1)


def middle_kernel(at, q, below, above, acc_in, top_in, total_in, acc, top, total):
    state = (acc, top, total)
    take((acc_in, top_in, total_in), state)
    q = q.at[0]
    y = at[0] // 2
    attend_chunk(q, [(below, ROWS)], state, y > 0)
    attend_chunk(q, [(above, ROWS)], state, y == 3)


def take(state_in, state):
    for src, dst in zip(state_in, state):
        dst[...] = src[...]


def far_kernel(at, q, fa, fb, acc_in, top_in, total_in, acc, top, total):
    state = (acc, top, total)
    take((acc_in, top_in, total_in), state)
    half = ROWS // 2
    attend_chunk(q.at[0], [(fa, half), (fb, half)], state, at[0] >= 4)


def end_kernel(at, q, fa, fb, acc_in, top_in, total_in, o0, o1, o2, o3, acc, top, total):
    far_kernel(at, q, fa, fb, acc_in, top_in, total_in, acc, top, total)
    for k, out in enumerate((o0, o1, o2, o3)):
        rows = pl.ds(pl.multiple_of(slot_of(at, k) * TOK, TAP), TOK)
        whole = jnp.sum(total[rows, :], axis=1, keepdims=True)
        out[...] = (acc[rows, :] / whole).astype(jnp.bfloat16)


STATE = [jax.ShapeDtypeStruct((ROWS, HD), jnp.float32)] * 3
UNIT_FLOPS = 4 * TOK * TOK * HD


def attend_call(kernel, name, units, outs, scratch, args):
    return pl.pallas_call(
        kernel,
        out_shape=outs,
        in_specs=[pl.BlockSpec(memory_space=pltpu.SMEM)] + [FULL] * (len(args) - 1),
        out_specs=[FULL] * len(outs),
        scratch_shapes=scratch,
        compiler_params=pltpu.CompilerParams(vmem_limit_bytes=LIMIT),
        cost_estimate=pl.CostEstimate(
            flops=2 * units * UNIT_FLOPS,
            bytes_accessed=6 * 2**20,
            transcendentals=units * TOK * TOK,
        ),
        name=name,
    )(*args)


def squares_kernel(p0, p1, p2, p3, out):
    wide = sum(jnp.square(p[...].astype(jnp.float32)) for p in (p0, p1, p2, p3))
    out[...] = jnp.sum(wide.T, axis=0, keepdims=True)


def norm_kernel(at, p0, p1, p2, p3, s0, s1, s2, s3, gain, out):
    power = (s0[...] + s1[...] + s2[...] + s3[...]) * (1.0 / CH)
    scale = jnp.broadcast_to(lax.rsqrt(power + 1e-6), (HD, TOK)).T
    for k, piece in enumerate((p0, p1, p2, p3)):
        cols = pl.ds(pl.multiple_of(lax.rem(at[2] + k, 4) * HD, HD), HD)
        out[:, cols] = (piece[...].astype(jnp.float32) * gain[:, cols] * scale).astype(jnp.bfloat16)


def local(streams, filters, gain):
    y, z, c = lax.axis_index("y"), lax.axis_index("z"), lax.axis_index("c")
    r = jnp.where(lax.rem(y, 2) == 0, z, 7 - z)
    at = jnp.stack([2 * y + c, z, y + r]).astype(jnp.int32)

    pieces = []
    for k in range(4):
        col = lax.rem(y + r + k, 4) * HD
        piece = lax.dynamic_slice(streams, (0, 0, col), (3, TOK, HD))
        pieces.append(send(piece, to_owner(k)))

    mine = lax.dynamic_slice(filters, (0, lax.rem(z, 4) * GH, 0), (3, GH, TAP))
    other = send(mine, swap_core)
    taps = jnp.where(c == z // 4, mine, other).reshape(3 * GH, TAP).astype(jnp.float32)
    table = make_tables(jnp.pad(taps[:, ::-1], ((0, 0), (1, TAP - 1))))
    tails = jnp.stack([p[:, TOK - TAP :, :] for p in pieces])
    up = send(tails, shift_owner(1))
    down = send(tails, shift_owner(-1))
    queries, own = filter_pieces(at, table, pieces, up, down)

    from_below = send(own, shift_y(1))
    from_above = send(own, shift_y(-1))
    partner = send(own, swap_core)
    state = attend_call(
        begin_kernel, "attend_begin", 18, STATE, [], (at, queries, own, partner)
    )
    half = ROWS // 2
    from_below, from_above, state = lax.optimization_barrier((from_below, from_above, state))
    far_a = send(from_below[:, :half], shift_y(1))
    far_b = send(from_above[:, half:], shift_y(-1))
    swapped_below = send(from_below, swap_core)
    swapped_above = send(from_above, swap_core)
    state = attend_call(
        middle_kernel, "attend_near", 16, STATE, [], (at, queries, from_below, from_above, *state)
    )
    state = attend_call(
        middle_kernel,
        "attend_swapped",
        16,
        STATE,
        [],
        (at, queries, swapped_below, swapped_above, *state),
    )
    far_a, far_b, state = lax.optimization_barrier((far_a, far_b, state))
    swapped_a = send(far_a, swap_core)
    swapped_b = send(far_b, swap_core)
    state = attend_call(far_kernel, "attend_far", 8, STATE, [], (at, queries, far_a, far_b, *state))
    pieces = attend_call(
        end_kernel,
        "attend_end",
        8,
        [jax.ShapeDtypeStruct((TOK, HD), jnp.bfloat16)] * 4,
        [pltpu.VMEM((ROWS, HD), jnp.float32)] * 3,
        (at, queries, swapped_a, swapped_b, *state),
    )

    home = [send_home(p, k) for k, p in enumerate(pieces)]
    part = pl.pallas_call(
        squares_kernel,
        out_shape=jax.ShapeDtypeStruct((1, TOK), jnp.float32),
        in_specs=[FULL] * 4,
        out_specs=FULL,
        name="squares",
    )(*home)
    part = part + send(part, swap_core)
    sums = [part] + [send(part, shift_x(i)) for i in (1, 2, 3)]
    return pl.pallas_call(
        norm_kernel,
        out_shape=jax.ShapeDtypeStruct((TOK, 4 * HD), jnp.bfloat16),
        in_specs=[pl.BlockSpec(memory_space=pltpu.SMEM)] + [FULL] * 9,
        out_specs=FULL,
        name="norm",
    )(at, *home, *sums, gain.reshape(1, 4 * HD))


def solution(mesh):
    split = Mesh(mesh.devices.reshape(NY, NZ, NX, NC), AXES)
    ctx, grp = ("y", "z"), ("x", "c")
    return jax.shard_map(
        local,
        mesh=split,
        in_specs=(P(None, ctx, grp), P(None, grp, None), P(grp)),
        out_specs=P(ctx, grp),
        check_vma=False,
    )
```

```python
import functools
import math

import jax
import jax.numpy as jnp
from jax import lax
from jax.experimental import pallas as pl
from jax.experimental.pallas import tpu as pltpu
from jax.sharding import Mesh
from jax.sharding import PartitionSpec as P

HD = 128
CH = 4096
NY, NZ, NX, NC = 4, 8, 4, 2
AXES = ("y", "z", "x", "c")
TOK = 384
TAP = 128
GW = 16
GH = HD // GW
ROWS = 4 * TOK
EXP2_SCALE = math.log2(math.e) / math.sqrt(HD)
FULL = pl.BlockSpec(memory_space=pltpu.VMEM)
LIMIT = 48 * 2**20


def linear(y, z, x, c):
    return ((y * NZ + z) * NX + x) * NC + c


def coords():
    for y in range(NY):
        for z in range(NZ):
            for x in range(NX):
                for c in range(NC):
                    yield y, z, x, c


def route(move):
    pairs = []
    for at in coords():
        to = move(*at)
        if to is not None:
            pairs.append((linear(*at), linear(*to)))
    return pairs


def send(block, move):
    return lax.ppermute(block, AXES, route(move))


def to_owner(step):
    def move(y, z, x, c):
        r = z if y % 2 == 0 else 7 - z
        return r // 2, 4 * c + (y + r + step) % 4, x, r % 2

    return move


def send_home(block, step):
    pairs = [(b, a) for a, b in route(to_owner(step))]
    return lax.ppermute(block, AXES, pairs)


def swap_core(y, z, x, c):
    return y, z, x, 1 - c


def shift_y(by):
    return lambda y, z, x, c: ((y + by) % NY, z, x, c)


def shift_x(by):
    return lambda y, z, x, c: (y, z, (x + by) % NX, c)


def shift_owner(by):
    def move(y, z, x, c):
        r = 2 * y + c + by
        return (r // 2, z, x, r % 2) if 0 <= r < 8 else None

    return move


def dot_nt(a, b):
    return lax.dot_general(a, b, (((1,), (1,)), ((), ())), preferred_element_type=jnp.float32)


def table_kernel(first_row, table):
    for i in range(3 * GH):
        row = jnp.broadcast_to(first_row[i : i + 1, :], (TAP, 2 * TAP))
        band = pltpu.roll(row, 0, 1, stride=1, stride_axis=0)
        table[i // GH, (i % GH) * TAP : (i % GH + 1) * TAP, :] = band.astype(jnp.bfloat16)


def make_tables(first_row):
    return pl.pallas_call(
        table_kernel,
        out_shape=jax.ShapeDtypeStruct((3, GH * TAP, 2 * TAP), jnp.bfloat16),
        in_specs=[FULL],
        out_specs=FULL,
        compiler_params=pltpu.CompilerParams(vmem_limit_bytes=LIMIT),
        name="tables",
    )(first_row)


def slot_of(at, k):
    return lax.rem(at[1] - at[0] - k + 16, 4)


def filter_kernel(at, table, p0, p1, p2, p3, up, down, q_out, kv_out):
    pieces = (p0, p1, p2, p3)
    r = at[0]
    lane_group = lax.broadcasted_iota(jnp.int32, (TAP, HD), 1) // GW
    slots = [slot_of(at, k) for k in range(4)]
    for s in range(3):
        out = q_out.at[0] if s == 0 else kv_out.at[s - 1]
        tiles = []
        for k, slot in enumerate(slots):
            own = jnp.logical_or(
                jnp.logical_and(slot == 2, r == 0),
                jnp.logical_and(lax.rem(slot, 2) == 1, r == 7),
            )
            before = jnp.where(
                own,
                pieces[(k + 1) % 4][s, TOK - TAP :, :],
                jnp.where(lax.rem(slot, 2) == 0, up[(k + 1) % 4, s], down[(k + 3) % 4, s]),
            )
            for t in range(TOK // TAP):
                now = pieces[k][s, t * TAP : (t + 1) * TAP, :]
                start = pl.multiple_of(slot * TOK + t * TAP, TAP)
                tiles.append((start, jnp.concatenate([before, now], axis=0)))
                before = now
        for i in range(0, len(tiles), 2):
            pair = jnp.concatenate([tiles[i][1], tiles[i + 1][1]], axis=1)
            wide = jnp.dot(table[s], pair, preferred_element_type=jnp.float32)
            for h in range(2):
                cols = slice(h * HD, (h + 1) * HD)
                res = wide[0:TAP, cols]
                for g in range(1, GH):
                    res = jnp.where(lane_group == g, wide[g * TAP : (g + 1) * TAP, cols], res)
                out[pl.ds(tiles[i + h][0], TAP), :] = res.astype(jnp.bfloat16)


def filter_pieces(at, table, pieces, up, down):
    return pl.pallas_call(
        filter_kernel,
        out_shape=[
            jax.ShapeDtypeStruct((1, ROWS, HD), jnp.bfloat16),
            jax.ShapeDtypeStruct((2, ROWS, HD), jnp.bfloat16),
        ],
        in_specs=[pl.BlockSpec(memory_space=pltpu.SMEM)] + [FULL] * 7,
        out_specs=[FULL] * 2,
        compiler_params=pltpu.CompilerParams(vmem_limit_bytes=LIMIT),
        name="filter",
    )(at, table, *pieces, up, down)


def attend_unit(scores, v, state, slot, diag, first):
    acc, top, total = state
    rows = slice(slot * TOK, (slot + 1) * TOK)
    cols = [
        piece[:, j * 128 : (j + 1) * 128] for piece in scores for j in range(piece.shape[1] // 128)
    ]
    if diag:
        row = lax.broadcasted_iota(jnp.int32, (TOK, 128), 0)
        col = lax.broadcasted_iota(jnp.int32, (TOK, 128), 1)
        for d in range(TOK // 128):
            j = len(cols) - TOK // 128 + d
            cols[j] = jnp.where(col + d * 128 <= row, cols[j], -1e30)
    high = functools.reduce(jnp.maximum, cols)
    high = jnp.broadcast_to(jnp.max(high, axis=1, keepdims=True), (TOK, 128))
    if not first:
        old = top[rows, :]
        high = jnp.maximum(old, high)
        fade = jnp.exp2((old - high) * EXP2_SCALE)
    weights = [jnp.exp2((s - high) * EXP2_SCALE) for s in cols]
    rounded = jnp.concatenate([w.astype(jnp.bfloat16) for w in weights], axis=1)
    added = functools.reduce(jnp.add, weights)
    res = None
    done = 0
    for values in v:
        size = values.shape[0]
        part = jnp.dot(
            rounded[:, done : done + size], values[...], preferred_element_type=jnp.float32
        )
        res = part if res is None else res + part
        done += size
    top[rows, :] = high
    if first:
        total[rows, :] = added
        acc[rows, :] = res
    else:
        total[rows, :] = total[rows, :] * fade + added
        acc[rows, :] = acc[rows, :] * fade + res


def attend_units(q, parts, state, lengths, diag=False, first=False):
    units = []
    for slot, left in enumerate(lengths):
        used = []
        for ref in parts:
            size = min(left, ref.shape[1])
            if size > 0:
                used.append((ref.at[0, 0:size, :], ref.at[1, 0:size, :]))
            left -= size
        if used:
            units.append((slot, used))

    def scores_of(unit):
        slot, used = unit
        rows = q[slot * TOK : (slot + 1) * TOK, :]
        return [dot_nt(rows, k[...]) for k, _ in used]

    scores = scores_of(units[0])
    for i, (slot, used) in enumerate(units):
        following = scores_of(units[i + 1]) if i + 1 < len(units) else None
        attend_unit(scores, [v for _, v in used], state, slot, diag, first)
        scores = following


def attend_chunk(q, parts, state, earlier):
    @pl.when(earlier)
    def _():
        attend_units(q, parts, state, (TOK, TOK, 3 * TOK, 3 * TOK))

    @pl.when(jnp.logical_not(earlier))
    def _():
        attend_units(q, parts, state, (0, 2 * TOK, 2 * TOK, 4 * TOK))


def begin_kernel(at, q, own, partner, acc, top, total):
    state = (acc, top, total)
    q = q.at[0]
    attend_units(q, [own], state, [(slot + 1) * TOK for slot in range(4)], diag=True, first=True)
    attend_chunk(q, [partner], state, lax.rem(at[0], 2) == 1)


def near_kernel(at, q, below, above, below_2, above_2, acc_in, top_in, total_in, acc, top, total):
    state = (acc, top, total)
    take((acc_in, top_in, total_in), state)
    q = q.at[0]
    y = at[0] // 2
    attend_chunk(q, [below], state, y > 0)
    attend_chunk(q, [above], state, y == 3)
    attend_chunk(q, [below_2], state, y > 0)
    attend_chunk(q, [above_2], state, y == 3)


def take(state_in, state):
    for src, dst in zip(state_in, state):
        dst[...] = src[...]


def far_kernel(at, q, fa, fb, acc_in, top_in, total_in, acc, top, total):
    state = (acc, top, total)
    take((acc_in, top_in, total_in), state)
    attend_chunk(q.at[0], [fa, fb], state, at[0] >= 4)


def end_kernel(at, q, fa, fb, acc_in, top_in, total_in, o0, o1, o2, o3, acc, top, total):
    state = (acc, top, total)
    take((acc_in, top_in, total_in), state)
    attend_chunk(q.at[0], [fa, fb], state, at[0] >= 4)
    for k, out in enumerate((o0, o1, o2, o3)):
        rows = pl.ds(pl.multiple_of(slot_of(at, k) * TOK, TAP), TOK)
        whole = jnp.sum(total[rows, :], axis=1, keepdims=True)
        out[...] = (acc[rows, :] / whole).astype(jnp.bfloat16)


STATE = [jax.ShapeDtypeStruct((ROWS, HD), jnp.float32)] * 3
UNIT_FLOPS = 4 * TOK * TOK * HD


def attend_call(kernel, name, units, outs, scratch, args):
    return pl.pallas_call(
        kernel,
        out_shape=outs,
        in_specs=[pl.BlockSpec(memory_space=pltpu.SMEM)] + [FULL] * (len(args) - 1),
        out_specs=[FULL] * len(outs),
        scratch_shapes=scratch,
        compiler_params=pltpu.CompilerParams(vmem_limit_bytes=LIMIT),
        cost_estimate=pl.CostEstimate(
            flops=2 * units * UNIT_FLOPS,
            bytes_accessed=6 * 2**20,
            transcendentals=units * TOK * TOK,
        ),
        name=name,
    )(*args)


def squares_kernel(p0, p1, p2, p3, out):
    wide = sum(jnp.square(p[...].astype(jnp.float32)) for p in (p0, p1, p2, p3))
    out[...] = jnp.sum(wide.T, axis=0, keepdims=True)


def norm_kernel(at, p0, p1, p2, p3, s0, s1, s2, s3, gain, out):
    power = (s0[...] + s1[...] + s2[...] + s3[...]) * (1.0 / CH)
    scale = jnp.broadcast_to(lax.rsqrt(power + 1e-6), (HD, TOK)).T
    for k, piece in enumerate((p0, p1, p2, p3)):
        cols = pl.ds(pl.multiple_of(lax.rem(at[2] + k, 4) * HD, HD), HD)
        out[:, cols] = (piece[...].astype(jnp.float32) * gain[:, cols] * scale).astype(jnp.bfloat16)


def local(streams, filters, gain):
    y, z, c = lax.axis_index("y"), lax.axis_index("z"), lax.axis_index("c")
    r = jnp.where(lax.rem(y, 2) == 0, z, 7 - z)
    at = jnp.stack([2 * y + c, z, y + r]).astype(jnp.int32)

    pieces = []
    for k in range(4):
        col = lax.rem(y + r + k, 4) * HD
        piece = lax.dynamic_slice(streams, (0, 0, col), (3, TOK, HD))
        pieces.append(send(piece, to_owner(k)))

    mine = lax.dynamic_slice(filters, (0, lax.rem(z, 4) * GH, 0), (3, GH, TAP))
    other = send(mine, swap_core)
    taps = jnp.where(c == z // 4, mine, other).reshape(3 * GH, TAP).astype(jnp.float32)
    table = make_tables(jnp.pad(taps[:, ::-1], ((0, 0), (1, TAP - 1))))
    tails = jnp.stack([p[:, TOK - TAP :, :] for p in pieces])
    up = send(tails, shift_owner(1))
    down = send(tails, shift_owner(-1))
    queries, own = filter_pieces(at, table, pieces, up, down)

    from_below = send(own, shift_y(1))
    from_above = send(own, shift_y(-1))
    partner = send(own, swap_core)
    state = attend_call(
        begin_kernel, "attend_begin", 18, STATE, [], (at, queries, own, partner)
    )
    half = ROWS // 2
    from_below, from_above, state = lax.optimization_barrier((from_below, from_above, state))
    far_a = send(from_below[:, :half], shift_y(1))
    far_b = send(from_above[:, half:], shift_y(-1))
    swapped_below = send(from_below, swap_core)
    swapped_above = send(from_above, swap_core)
    state = attend_call(
        near_kernel,
        "attend_near",
        32,
        STATE,
        [],
        (at, queries, from_below, from_above, swapped_below, swapped_above, *state),
    )
    far_a, far_b, state = lax.optimization_barrier((far_a, far_b, state))
    swapped_a = send(far_a, swap_core)
    swapped_b = send(far_b, swap_core)
    state = attend_call(far_kernel, "attend_far", 8, STATE, [], (at, queries, far_a, far_b, *state))
    pieces = attend_call(
        end_kernel,
        "attend_end",
        8,
        [jax.ShapeDtypeStruct((TOK, HD), jnp.bfloat16)] * 4,
        [pltpu.VMEM((ROWS, HD), jnp.float32)] * 3,
        (at, queries, swapped_a, swapped_b, *state),
    )

    home = [send_home(p, k) for k, p in enumerate(pieces)]
    part = pl.pallas_call(
        squares_kernel,
        out_shape=jax.ShapeDtypeStruct((1, TOK), jnp.float32),
        in_specs=[FULL] * 4,
        out_specs=FULL,
        name="squares",
    )(*home)
    part = part + send(part, swap_core)
    sums = [part] + [send(part, shift_x(i)) for i in (1, 2, 3)]
    return pl.pallas_call(
        norm_kernel,
        out_shape=jax.ShapeDtypeStruct((TOK, 4 * HD), jnp.bfloat16),
        in_specs=[pl.BlockSpec(memory_space=pltpu.SMEM)] + [FULL] * 9,
        out_specs=FULL,
        name="norm",
    )(at, *home, *sums, gain.reshape(1, 4 * HD))


def solution(mesh):
    split = Mesh(mesh.devices.reshape(NY, NZ, NX, NC), AXES)
    ctx, grp = ("y", "z"), ("x", "c")
    return jax.shard_map(
        local,
        mesh=split,
        in_specs=(P(None, ctx, grp), P(None, grp, None), P(grp)),
        out_specs=P(ctx, grp),
        check_vma=False,
    )
```

```python
import functools
import math

import jax
import jax.numpy as jnp
from jax import lax
from jax.experimental import pallas as pl
from jax.experimental.pallas import tpu as pltpu
from jax.sharding import Mesh
from jax.sharding import PartitionSpec as P

HD = 128
CH = 4096
NY, NZ, NX, NC = 4, 8, 4, 2
AXES = ("y", "z", "x", "c")
TOK = 384
TAP = 128
GW = 16
GH = HD // GW
ROWS = 4 * TOK
EXP2_SCALE = math.log2(math.e) / math.sqrt(HD)
FULL = pl.BlockSpec(memory_space=pltpu.VMEM)
LIMIT = 48 * 2**20


def linear(y, z, x, c):
    return ((y * NZ + z) * NX + x) * NC + c


def coords():
    for y in range(NY):
        for z in range(NZ):
            for x in range(NX):
                for c in range(NC):
                    yield y, z, x, c


def route(move):
    pairs = []
    for at in coords():
        to = move(*at)
        if to is not None:
            pairs.append((linear(*at), linear(*to)))
    return pairs


def send(block, move):
    return lax.ppermute(block, AXES, route(move))


def to_owner(step):
    def move(y, z, x, c):
        r = z if y % 2 == 0 else 7 - z
        return r // 2, 4 * c + (y + r + step) % 4, x, r % 2

    return move


def send_home(block, step):
    pairs = [(b, a) for a, b in route(to_owner(step))]
    return lax.ppermute(block, AXES, pairs)


def swap_core(y, z, x, c):
    return y, z, x, 1 - c


def shift_y(by):
    return lambda y, z, x, c: ((y + by) % NY, z, x, c)


def shift_x(by):
    return lambda y, z, x, c: (y, z, (x + by) % NX, c)


def shift_owner(by):
    def move(y, z, x, c):
        r = 2 * y + c + by
        return (r // 2, z, x, r % 2) if 0 <= r < 8 else None

    return move


def dot_nt(a, b):
    return lax.dot_general(a, b, (((1,), (1,)), ((), ())), preferred_element_type=jnp.float32)


def table_kernel(first_row, table):
    for i in range(3 * GH):
        row = jnp.broadcast_to(first_row[i : i + 1, :], (TAP, 2 * TAP))
        band = pltpu.roll(row, 0, 1, stride=1, stride_axis=0)
        table[i // GH, (i % GH) * TAP : (i % GH + 1) * TAP, :] = band.astype(jnp.bfloat16)


def make_tables(first_row):
    return pl.pallas_call(
        table_kernel,
        out_shape=jax.ShapeDtypeStruct((3, GH * TAP, 2 * TAP), jnp.bfloat16),
        in_specs=[FULL],
        out_specs=FULL,
        compiler_params=pltpu.CompilerParams(vmem_limit_bytes=LIMIT),
        name="tables",
    )(first_row)


def slot_of(at, k):
    return lax.rem(at[1] - at[0] - k + 16, 4)


def filter_kernel(at, table, p0, p1, p2, p3, up, down, q_out, kv_out):
    pieces = (p0, p1, p2, p3)
    r = at[0]
    lane_group = lax.broadcasted_iota(jnp.int32, (TAP, HD), 1) // GW
    slots = [slot_of(at, k) for k in range(4)]
    for s in range(3):
        out = q_out.at[0] if s == 0 else kv_out.at[s - 1]
        tiles = []
        for k, slot in enumerate(slots):
            own = jnp.logical_or(
                jnp.logical_and(slot == 2, r == 0),
                jnp.logical_and(lax.rem(slot, 2) == 1, r == 7),
            )
            before = jnp.where(
                own,
                pieces[(k + 1) % 4][s, TOK - TAP :, :],
                jnp.where(lax.rem(slot, 2) == 0, up[(k + 1) % 4, s], down[(k + 3) % 4, s]),
            )
            for t in range(TOK // TAP):
                now = pieces[k][s, t * TAP : (t + 1) * TAP, :]
                start = pl.multiple_of(slot * TOK + t * TAP, TAP)
                tiles.append((start, jnp.concatenate([before, now], axis=0)))
                before = now
        for i in range(0, len(tiles), 2):
            pair = jnp.concatenate([tiles[i][1], tiles[i + 1][1]], axis=1)
            wide = jnp.dot(table[s], pair, preferred_element_type=jnp.float32)
            for h in range(2):
                cols = slice(h * HD, (h + 1) * HD)
                res = wide[0:TAP, cols]
                for g in range(1, GH):
                    res = jnp.where(lane_group == g, wide[g * TAP : (g + 1) * TAP, cols], res)
                out[pl.ds(tiles[i + h][0], TAP), :] = res.astype(jnp.bfloat16)


def filter_pieces(at, table, pieces, up, down):
    return pl.pallas_call(
        filter_kernel,
        out_shape=[
            jax.ShapeDtypeStruct((1, ROWS, HD), jnp.bfloat16),
            jax.ShapeDtypeStruct((2, ROWS, HD), jnp.bfloat16),
        ],
        in_specs=[pl.BlockSpec(memory_space=pltpu.SMEM)] + [FULL] * 7,
        out_specs=[FULL] * 2,
        compiler_params=pltpu.CompilerParams(vmem_limit_bytes=LIMIT),
        name="filter",
    )(at, table, *pieces, up, down)


def attend_unit(scores, v, state, slot, diag, first):
    acc, top, total = state
    rows = slice(slot * TOK, (slot + 1) * TOK)
    cols = [
        piece[:, j * 128 : (j + 1) * 128] for piece in scores for j in range(piece.shape[1] // 128)
    ]
    if diag:
        row = lax.broadcasted_iota(jnp.int32, (TOK, 128), 0)
        col = lax.broadcasted_iota(jnp.int32, (TOK, 128), 1)
        for d in range(TOK // 128):
            j = len(cols) - TOK // 128 + d
            cols[j] = jnp.where(col + d * 128 <= row, cols[j], -1e30)
    high = functools.reduce(jnp.maximum, cols)
    high = jnp.broadcast_to(jnp.max(high, axis=1, keepdims=True), (TOK, 128))
    if not first:
        old = top[rows, :]
        high = jnp.maximum(old, high)
        fade = jnp.exp2((old - high) * EXP2_SCALE)
    weights = [jnp.exp2((s - high) * EXP2_SCALE) for s in cols]
    rounded = jnp.concatenate([w.astype(jnp.bfloat16) for w in weights], axis=1)
    added = functools.reduce(jnp.add, weights)
    res = None
    done = 0
    for values in v:
        size = values.shape[0]
        part = jnp.dot(
            rounded[:, done : done + size], values[...], preferred_element_type=jnp.float32
        )
        res = part if res is None else res + part
        done += size
    top[rows, :] = high
    if first:
        total[rows, :] = added
        acc[rows, :] = res
    else:
        total[rows, :] = total[rows, :] * fade + added
        acc[rows, :] = acc[rows, :] * fade + res


def attend_units(q, chunks, state, lengths, diag=False, first=False):
    units = []
    for slot, length in enumerate(lengths):
        used = []
        for parts in chunks:
            left = length
            for ref in parts:
                size = min(left, ref.shape[1])
                if size > 0:
                    used.append((ref.at[0, 0:size, :], ref.at[1, 0:size, :]))
                left -= size
        if used:
            units.append((slot, used))

    def scores_of(unit):
        slot, used = unit
        rows = q[slot * TOK : (slot + 1) * TOK, :]
        return [dot_nt(rows, k[...]) for k, _ in used]

    scores = scores_of(units[0])
    for i, (slot, used) in enumerate(units):
        following = scores_of(units[i + 1]) if i + 1 < len(units) else None
        attend_unit(scores, [v for _, v in used], state, slot, diag, first)
        scores = following


def attend_chunks(q, chunks, state, earlier):
    @pl.when(earlier)
    def _():
        attend_units(q, chunks, state, (TOK, TOK, 3 * TOK, 3 * TOK))

    @pl.when(jnp.logical_not(earlier))
    def _():
        attend_units(q, chunks, state, (0, 2 * TOK, 2 * TOK, 4 * TOK))


def begin_kernel(at, q, own, partner, acc, top, total):
    state = (acc, top, total)
    q = q.at[0]
    attend_units(q, [[own]], state, [(slot + 1) * TOK for slot in range(4)], diag=True, first=True)
    attend_chunks(q, [[partner]], state, lax.rem(at[0], 2) == 1)


def near_kernel(at, q, below, above, below_2, above_2, acc_in, top_in, total_in, acc, top, total):
    state = (acc, top, total)
    take((acc_in, top_in, total_in), state)
    q = q.at[0]
    y = at[0] // 2
    attend_chunks(q, [[below], [below_2]], state, y > 0)
    attend_chunks(q, [[above], [above_2]], state, y == 3)


def take(state_in, state):
    for src, dst in zip(state_in, state):
        dst[...] = src[...]


def far_kernel(at, q, fa, fb, acc_in, top_in, total_in, acc, top, total):
    state = (acc, top, total)
    take((acc_in, top_in, total_in), state)
    attend_chunks(q.at[0], [[fa, fb]], state, at[0] >= 4)


def end_kernel(at, q, fa, fb, acc_in, top_in, total_in, o0, o1, o2, o3, acc, top, total):
    state = (acc, top, total)
    take((acc_in, top_in, total_in), state)
    attend_chunks(q.at[0], [[fa, fb]], state, at[0] >= 4)
    for k, out in enumerate((o0, o1, o2, o3)):
        rows = pl.ds(pl.multiple_of(slot_of(at, k) * TOK, TAP), TOK)
        whole = jnp.sum(total[rows, :], axis=1, keepdims=True)
        out[...] = (acc[rows, :] / whole).astype(jnp.bfloat16)


STATE = [jax.ShapeDtypeStruct((ROWS, HD), jnp.float32)] * 3
UNIT_FLOPS = 4 * TOK * TOK * HD


def attend_call(kernel, name, units, outs, scratch, args):
    return pl.pallas_call(
        kernel,
        out_shape=outs,
        in_specs=[pl.BlockSpec(memory_space=pltpu.SMEM)] + [FULL] * (len(args) - 1),
        out_specs=[FULL] * len(outs),
        scratch_shapes=scratch,
        compiler_params=pltpu.CompilerParams(vmem_limit_bytes=LIMIT),
        cost_estimate=pl.CostEstimate(
            flops=2 * units * UNIT_FLOPS,
            bytes_accessed=6 * 2**20,
            transcendentals=units * TOK * TOK,
        ),
        name=name,
    )(*args)


def squares_kernel(p0, p1, p2, p3, out):
    wide = sum(jnp.square(p[...].astype(jnp.float32)) for p in (p0, p1, p2, p3))
    ones = jnp.ones((8, HD), jnp.float32)
    sums = lax.dot_general(
        ones, wide, (((1,), (1,)), ((), ())), precision=lax.Precision.HIGHEST,
        preferred_element_type=jnp.float32,
    )
    out[...] = sums[0:1, :]


def norm_kernel(at, p0, p1, p2, p3, s0, s1, s2, s3, gain, out):
    power = (s0[...] + s1[...] + s2[...] + s3[...]) * (1.0 / CH)
    scale = jnp.broadcast_to(lax.rsqrt(power + 1e-6), (HD, TOK)).T
    for k, piece in enumerate((p0, p1, p2, p3)):
        cols = pl.ds(pl.multiple_of(lax.rem(at[2] + k, 4) * HD, HD), HD)
        out[:, cols] = (piece[...].astype(jnp.float32) * gain[:, cols] * scale).astype(jnp.bfloat16)


def local(streams, filters, gain):
    y, z, c = lax.axis_index("y"), lax.axis_index("z"), lax.axis_index("c")
    r = jnp.where(lax.rem(y, 2) == 0, z, 7 - z)
    at = jnp.stack([2 * y + c, z, y + r]).astype(jnp.int32)

    pieces = []
    for k in range(4):
        col = lax.rem(y + r + k, 4) * HD
        piece = lax.dynamic_slice(streams, (0, 0, col), (3, TOK, HD))
        pieces.append(send(piece, to_owner(k)))

    mine = lax.dynamic_slice(filters, (0, lax.rem(z, 4) * GH, 0), (3, GH, TAP))
    other = send(mine, swap_core)
    taps = jnp.where(c == z // 4, mine, other).reshape(3 * GH, TAP).astype(jnp.float32)
    table = make_tables(jnp.pad(taps[:, ::-1], ((0, 0), (1, TAP - 1))))
    tails = jnp.stack([p[:, TOK - TAP :, :] for p in pieces])
    tails, table = lax.optimization_barrier((tails, table))
    up = send(tails, shift_owner(1))
    down = send(tails, shift_owner(-1))
    queries, own = filter_pieces(at, table, pieces, up, down)

    from_below = send(own, shift_y(1))
    from_above = send(own, shift_y(-1))
    partner = send(own, swap_core)
    state = attend_call(
        begin_kernel, "attend_begin", 18, STATE, [], (at, queries, own, partner)
    )
    half = ROWS // 2
    from_below, from_above, state = lax.optimization_barrier((from_below, from_above, state))
    far_a = send(from_below[:, :half], shift_y(1))
    far_b = send(from_above[:, half:], shift_y(-1))
    swapped_below = send(from_below, swap_core)
    swapped_above = send(from_above, swap_core)
    state = attend_call(
        near_kernel,
        "attend_near",
        32,
        STATE,
        [],
        (at, queries, from_below, from_above, swapped_below, swapped_above, *state),
    )
    far_a, far_b, state = lax.optimization_barrier((far_a, far_b, state))
    swapped_a = send(far_a, swap_core)
    swapped_b = send(far_b, swap_core)
    state = attend_call(far_kernel, "attend_far", 8, STATE, [], (at, queries, far_a, far_b, *state))
    pieces = attend_call(
        end_kernel,
        "attend_end",
        8,
        [jax.ShapeDtypeStruct((TOK, HD), jnp.bfloat16)] * 4,
        [pltpu.VMEM((ROWS, HD), jnp.float32)] * 3,
        (at, queries, swapped_a, swapped_b, *state),
    )

    home = [send_home(p, k) for k, p in enumerate(pieces)]
    part = pl.pallas_call(
        squares_kernel,
        out_shape=jax.ShapeDtypeStruct((1, TOK), jnp.float32),
        in_specs=[FULL] * 4,
        out_specs=FULL,
        name="squares",
    )(*home)
    part = part + send(part, swap_core)
    sums = [part] + [send(part, shift_x(i)) for i in (1, 2, 3)]
    return pl.pallas_call(
        norm_kernel,
        out_shape=jax.ShapeDtypeStruct((TOK, 4 * HD), jnp.bfloat16),
        in_specs=[pl.BlockSpec(memory_space=pltpu.SMEM)] + [FULL] * 9,
        out_specs=FULL,
        name="norm",
    )(at, *home, *sums, gain.reshape(1, 4 * HD))


def solution(mesh):
    split = Mesh(mesh.devices.reshape(NY, NZ, NX, NC), AXES)
    ctx, grp = ("y", "z"), ("x", "c")
    return jax.shard_map(
        local,
        mesh=split,
        in_specs=(P(None, ctx, grp), P(None, grp, None), P(grp)),
        out_specs=P(ctx, grp),
        check_vma=False,
    )
```

```python
import functools
import math

import jax
import jax.numpy as jnp
from jax import lax
from jax.experimental import pallas as pl
from jax.experimental.pallas import tpu as pltpu
from jax.sharding import Mesh
from jax.sharding import PartitionSpec as P

HD = 128
CH = 4096
NY, NZ, NX, NC = 4, 8, 4, 2
AXES = ("y", "z", "x", "c")
TOK = 384
TAP = 128
GW = 16
GH = HD // GW
ROWS = 4 * TOK
EXP2_SCALE = math.log2(math.e) / math.sqrt(HD)
FULL = pl.BlockSpec(memory_space=pltpu.VMEM)
LIMIT = 48 * 2**20


def linear(y, z, x, c):
    return ((y * NZ + z) * NX + x) * NC + c


def coords():
    for y in range(NY):
        for z in range(NZ):
            for x in range(NX):
                for c in range(NC):
                    yield y, z, x, c


def route(move):
    pairs = []
    for at in coords():
        to = move(*at)
        if to is not None:
            pairs.append((linear(*at), linear(*to)))
    return pairs


def send(block, move):
    return lax.ppermute(block, AXES, route(move))


def to_owner(step):
    def move(y, z, x, c):
        r = z if y % 2 == 0 else 7 - z
        return r // 2, 4 * c + (y + r + step) % 4, x, r % 2

    return move


def send_home(block, step):
    pairs = [(b, a) for a, b in route(to_owner(step))]
    return lax.ppermute(block, AXES, pairs)


def swap_core(y, z, x, c):
    return y, z, x, 1 - c


def shift_y(by):
    return lambda y, z, x, c: ((y + by) % NY, z, x, c)


def shift_x(by):
    return lambda y, z, x, c: (y, z, (x + by) % NX, c)


def shift_owner(by):
    def move(y, z, x, c):
        r = 2 * y + c + by
        return (r // 2, z, x, r % 2) if 0 <= r < 8 else None

    return move


def dot_nt(a, b):
    return lax.dot_general(a, b, (((1,), (1,)), ((), ())), preferred_element_type=jnp.float32)


def table_kernel(first_row, table):
    for i in range(3 * GH):
        row = jnp.broadcast_to(first_row[i : i + 1, :], (TAP, 2 * TAP))
        band = pltpu.roll(row, 0, 1, stride=1, stride_axis=0)
        table[i // GH, (i % GH) * TAP : (i % GH + 1) * TAP, :] = band.astype(jnp.bfloat16)


def make_tables(first_row):
    return pl.pallas_call(
        table_kernel,
        out_shape=jax.ShapeDtypeStruct((3, GH * TAP, 2 * TAP), jnp.bfloat16),
        in_specs=[FULL],
        out_specs=FULL,
        compiler_params=pltpu.CompilerParams(vmem_limit_bytes=LIMIT),
        name="tables",
    )(first_row)


def slot_of(at, k):
    return lax.rem(at[1] - at[0] - k + 16, 4)


def filter_kernel(at, table, p0, p1, p2, p3, up, down, q_out, kv_out):
    pieces = (p0, p1, p2, p3)
    r = at[0]
    lane_group = lax.broadcasted_iota(jnp.int32, (TAP, HD), 1) // GW
    slots = [slot_of(at, k) for k in range(4)]
    for s in range(3):
        out = q_out.at[0] if s == 0 else kv_out.at[s - 1]
        tiles = []
        for k, slot in enumerate(slots):
            ahead = at[1] - r + 16
            from_up = lax.rem(ahead + 1 - lax.rem(ahead + 1, 2) - slot, 4) // 2
            from_down = lax.rem(ahead - 2 + lax.rem(ahead - 1, 2) - slot, 4) // 2
            own = jnp.logical_or(
                jnp.logical_and(slot == 2, r == 0),
                jnp.logical_and(lax.rem(slot, 2) == 1, r == 7),
            )
            before = jnp.where(
                own,
                pieces[(k + 1) % 4][s, TOK - TAP :, :],
                jnp.where(lax.rem(slot, 2) == 0, up[from_up, s], down[from_down, s]),
            )
            for t in range(TOK // TAP):
                now = pieces[k][s, t * TAP : (t + 1) * TAP, :]
                start = pl.multiple_of(slot * TOK + t * TAP, TAP)
                tiles.append((start, jnp.concatenate([before, now], axis=0)))
                before = now
        for i in range(0, len(tiles), 2):
            pair = jnp.concatenate([tiles[i][1], tiles[i + 1][1]], axis=1)
            wide = jnp.dot(table[s], pair, preferred_element_type=jnp.float32)
            for h in range(2):
                cols = slice(h * HD, (h + 1) * HD)
                res = wide[0:TAP, cols]
                for g in range(1, GH):
                    res = jnp.where(lane_group == g, wide[g * TAP : (g + 1) * TAP, cols], res)
                out[pl.ds(tiles[i + h][0], TAP), :] = res.astype(jnp.bfloat16)


def filter_pieces(at, table, pieces, up, down):
    return pl.pallas_call(
        filter_kernel,
        out_shape=[
            jax.ShapeDtypeStruct((1, ROWS, HD), jnp.bfloat16),
            jax.ShapeDtypeStruct((2, ROWS, HD), jnp.bfloat16),
        ],
        in_specs=[pl.BlockSpec(memory_space=pltpu.SMEM)] + [FULL] * 7,
        out_specs=[FULL] * 2,
        compiler_params=pltpu.CompilerParams(vmem_limit_bytes=LIMIT),
        name="filter",
    )(at, table, *pieces, up, down)


def attend_unit(scores, v, state, slot, diag, first):
    acc, top, total = state
    rows = slice(slot * TOK, (slot + 1) * TOK)
    cols = [
        piece[:, j * 128 : (j + 1) * 128] for piece in scores for j in range(piece.shape[1] // 128)
    ]
    if diag:
        row = lax.broadcasted_iota(jnp.int32, (TOK, 128), 0)
        col = lax.broadcasted_iota(jnp.int32, (TOK, 128), 1)
        for d in range(TOK // 128):
            j = len(cols) - TOK // 128 + d
            cols[j] = jnp.where(col + d * 128 <= row, cols[j], -1e30)
    high = functools.reduce(jnp.maximum, cols)
    high = jnp.broadcast_to(jnp.max(high, axis=1, keepdims=True), (TOK, 128))
    if not first:
        old = top[rows, :]
        high = jnp.maximum(old, high)
        fade = jnp.exp2((old - high) * EXP2_SCALE)
    weights = [jnp.exp2((s - high) * EXP2_SCALE) for s in cols]
    rounded = jnp.concatenate([w.astype(jnp.bfloat16) for w in weights], axis=1)
    added = functools.reduce(jnp.add, weights)
    res = None
    done = 0
    for values in v:
        size = values.shape[0]
        part = jnp.dot(
            rounded[:, done : done + size], values[...], preferred_element_type=jnp.float32
        )
        res = part if res is None else res + part
        done += size
    top[rows, :] = high
    if first:
        total[rows, :] = added
        acc[rows, :] = res
    else:
        total[rows, :] = total[rows, :] * fade + added
        acc[rows, :] = acc[rows, :] * fade + res


def attend_units(q, chunks, state, lengths, diag=False, first=False):
    units = []
    for slot, length in enumerate(lengths):
        used = []
        for parts in chunks:
            left = length
            for ref in parts:
                size = min(left, ref.shape[1])
                if size > 0:
                    used.append((ref.at[0, 0:size, :], ref.at[1, 0:size, :]))
                left -= size
        if used:
            units.append((slot, used))

    def scores_of(unit):
        slot, used = unit
        rows = q[slot * TOK : (slot + 1) * TOK, :]
        return [dot_nt(rows, k[...]) for k, _ in used]

    scores = scores_of(units[0])
    for i, (slot, used) in enumerate(units):
        following = scores_of(units[i + 1]) if i + 1 < len(units) else None
        attend_unit(scores, [v for _, v in used], state, slot, diag, first)
        scores = following


def attend_chunks(q, chunks, state, earlier):
    @pl.when(earlier)
    def _():
        attend_units(q, chunks, state, (TOK, TOK, 3 * TOK, 3 * TOK))

    @pl.when(jnp.logical_not(earlier))
    def _():
        attend_units(q, chunks, state, (0, 2 * TOK, 2 * TOK, 4 * TOK))


def begin_kernel(at, q, own, partner, acc, top, total):
    state = (acc, top, total)
    q = q.at[0]
    attend_units(q, [[own]], state, [(slot + 1) * TOK for slot in range(4)], diag=True, first=True)
    attend_chunks(q, [[partner]], state, lax.rem(at[0], 2) == 1)


def near_kernel(at, q, below, above, below_2, above_2, acc_in, top_in, total_in, acc, top, total):
    state = (acc, top, total)
    take((acc_in, top_in, total_in), state)
    q = q.at[0]
    y = at[0] // 2
    attend_chunks(q, [[below], [below_2]], state, y > 0)
    attend_chunks(q, [[above], [above_2]], state, y == 3)


def take(state_in, state):
    for src, dst in zip(state_in, state):
        dst[...] = src[...]


def far_kernel(at, q, fa, fb, acc_in, top_in, total_in, acc, top, total):
    state = (acc, top, total)
    take((acc_in, top_in, total_in), state)
    attend_chunks(q.at[0], [[fa, fb]], state, at[0] >= 4)


def end_kernel(at, q, fa, fb, acc_in, top_in, total_in, o0, o1, o2, o3, acc, top, total):
    state = (acc, top, total)
    take((acc_in, top_in, total_in), state)
    attend_chunks(q.at[0], [[fa, fb]], state, at[0] >= 4)
    for k, out in enumerate((o0, o1, o2, o3)):
        rows = pl.ds(pl.multiple_of(slot_of(at, k) * TOK, TAP), TOK)
        whole = jnp.sum(total[rows, :], axis=1, keepdims=True)
        out[...] = (acc[rows, :] / whole).astype(jnp.bfloat16)


STATE = [jax.ShapeDtypeStruct((ROWS, HD), jnp.float32)] * 3
UNIT_FLOPS = 4 * TOK * TOK * HD


def attend_call(kernel, name, units, outs, scratch, args):
    return pl.pallas_call(
        kernel,
        out_shape=outs,
        in_specs=[pl.BlockSpec(memory_space=pltpu.SMEM)] + [FULL] * (len(args) - 1),
        out_specs=[FULL] * len(outs),
        scratch_shapes=scratch,
        compiler_params=pltpu.CompilerParams(vmem_limit_bytes=LIMIT),
        cost_estimate=pl.CostEstimate(
            flops=2 * units * UNIT_FLOPS,
            bytes_accessed=6 * 2**20,
            transcendentals=units * TOK * TOK,
        ),
        name=name,
    )(*args)


def squares_kernel(p0, p1, p2, p3, out):
    wide = sum(jnp.square(p[...].astype(jnp.float32)) for p in (p0, p1, p2, p3))
    out[...] = jnp.sum(wide.T, axis=0, keepdims=True)


def norm_kernel(at, p0, p1, p2, p3, s0, s1, s2, s3, gain, out):
    power = (s0[...] + s1[...] + s2[...] + s3[...]) * (1.0 / CH)
    scale = jnp.broadcast_to(lax.rsqrt(power + 1e-6), (HD, TOK)).T
    for k, piece in enumerate((p0, p1, p2, p3)):
        cols = pl.ds(pl.multiple_of(lax.rem(at[2] + k, 4) * HD, HD), HD)
        out[:, cols] = (piece[...].astype(jnp.float32) * gain[:, cols] * scale).astype(jnp.bfloat16)


def local(streams, filters, gain):
    y, z, c = lax.axis_index("y"), lax.axis_index("z"), lax.axis_index("c")
    r = jnp.where(lax.rem(y, 2) == 0, z, 7 - z)
    at = jnp.stack([2 * y + c, z, y + r]).astype(jnp.int32)

    pieces = []
    for k in range(4):
        col = lax.rem(y + r + k, 4) * HD
        piece = lax.dynamic_slice(streams, (0, 0, col), (3, TOK, HD))
        pieces.append(send(piece, to_owner(k)))

    mine = lax.dynamic_slice(filters, (0, lax.rem(z, 4) * GH, 0), (3, GH, TAP))
    other = send(mine, swap_core)
    taps = jnp.where(c == z // 4, mine, other).reshape(3 * GH, TAP).astype(jnp.float32)
    table = make_tables(jnp.pad(taps[:, ::-1], ((0, 0), (1, TAP - 1))))
    t0, t1, t2, t3 = (p[:, TOK - TAP :, :] for p in pieces)
    flip = lax.rem(z + c, 2) == 1
    up = send(jnp.where(flip, jnp.stack([t1, t3]), jnp.stack([t0, t2])), shift_owner(1))
    down = send(jnp.where(flip, jnp.stack([t0, t2]), jnp.stack([t1, t3])), shift_owner(-1))
    queries, own = filter_pieces(at, table, pieces, up, down)

    from_below = send(own, shift_y(1))
    from_above = send(own, shift_y(-1))
    partner = send(own, swap_core)
    state = attend_call(
        begin_kernel, "attend_begin", 18, STATE, [], (at, queries, own, partner)
    )
    half = ROWS // 2
    from_below, from_above, state = lax.optimization_barrier((from_below, from_above, state))
    far_a = send(from_below[:, :half], shift_y(1))
    far_b = send(from_above[:, half:], shift_y(-1))
    swapped_below = send(from_below, swap_core)
    swapped_above = send(from_above, swap_core)
    state = attend_call(
        near_kernel,
        "attend_near",
        32,
        STATE,
        [],
        (at, queries, from_below, from_above, swapped_below, swapped_above, *state),
    )
    far_a, far_b, state = lax.optimization_barrier((far_a, far_b, state))
    swapped_a = send(far_a, swap_core)
    swapped_b = send(far_b, swap_core)
    state = attend_call(far_kernel, "attend_far", 8, STATE, [], (at, queries, far_a, far_b, *state))
    pieces = attend_call(
        end_kernel,
        "attend_end",
        8,
        [jax.ShapeDtypeStruct((TOK, HD), jnp.bfloat16)] * 4,
        [pltpu.VMEM((ROWS, HD), jnp.float32)] * 3,
        (at, queries, swapped_a, swapped_b, *state),
    )

    home = [send_home(p, k) for k, p in enumerate(pieces)]
    part = pl.pallas_call(
        squares_kernel,
        out_shape=jax.ShapeDtypeStruct((1, TOK), jnp.float32),
        in_specs=[FULL] * 4,
        out_specs=FULL,
        name="squares",
    )(*home)
    part = part + send(part, swap_core)
    sums = [part] + [send(part, shift_x(i)) for i in (1, 2, 3)]
    return pl.pallas_call(
        norm_kernel,
        out_shape=jax.ShapeDtypeStruct((TOK, 4 * HD), jnp.bfloat16),
        in_specs=[pl.BlockSpec(memory_space=pltpu.SMEM)] + [FULL] * 9,
        out_specs=FULL,
        name="norm",
    )(at, *home, *sums, gain.reshape(1, 4 * HD))


def solution(mesh):
    split = Mesh(mesh.devices.reshape(NY, NZ, NX, NC), AXES)
    ctx, grp = ("y", "z"), ("x", "c")
    return jax.shard_map(
        local,
        mesh=split,
        in_specs=(P(None, ctx, grp), P(None, grp, None), P(grp)),
        out_specs=P(ctx, grp),
        check_vma=False,
    )
```

```python
import functools
import math

import jax
import jax.numpy as jnp
from jax import lax
from jax.experimental import pallas as pl
from jax.experimental.pallas import tpu as pltpu
from jax.sharding import Mesh
from jax.sharding import PartitionSpec as P

HD = 128
CH = 4096
NY, NZ, NX, NC = 4, 8, 4, 2
AXES = ("y", "z", "x", "c")
TOK = 384
TAP = 128
GW = 16
GH = HD // GW
ROWS = 4 * TOK
EXP2_SCALE = math.log2(math.e) / math.sqrt(HD)
FULL = pl.BlockSpec(memory_space=pltpu.VMEM)
LIMIT = 48 * 2**20


def linear(y, z, x, c):
    return ((y * NZ + z) * NX + x) * NC + c


def coords():
    for y in range(NY):
        for z in range(NZ):
            for x in range(NX):
                for c in range(NC):
                    yield y, z, x, c


def route(move):
    pairs = []
    for at in coords():
        to = move(*at)
        if to is not None:
            pairs.append((linear(*at), linear(*to)))
    return pairs


def send(block, move):
    return lax.ppermute(block, AXES, route(move))


def to_owner(step):
    def move(y, z, x, c):
        r = z if y % 2 == 0 else 7 - z
        return r // 2, 4 * c + (y + r + step) % 4, x, r % 2

    return move


def send_home(block, step):
    pairs = [(b, a) for a, b in route(to_owner(step))]
    return lax.ppermute(block, AXES, pairs)


def swap_core(y, z, x, c):
    return y, z, x, 1 - c


def shift_y(by):
    return lambda y, z, x, c: ((y + by) % NY, z, x, c)


def shift_x(by):
    return lambda y, z, x, c: (y, z, (x + by) % NX, c)


def shift_owner(by):
    def move(y, z, x, c):
        r = 2 * y + c + by
        return (r // 2, z, x, r % 2) if 0 <= r < 8 else None

    return move


def dot_nt(a, b):
    return lax.dot_general(a, b, (((1,), (1,)), ((), ())), preferred_element_type=jnp.float32)


def table_kernel(first_row, table):
    for i in range(3 * GH):
        row = jnp.broadcast_to(first_row[i : i + 1, :], (TAP, 2 * TAP))
        band = pltpu.roll(row, 0, 1, stride=1, stride_axis=0)
        table[i // GH, (i % GH) * TAP : (i % GH + 1) * TAP, :] = band.astype(jnp.bfloat16)


def make_tables(first_row):
    return pl.pallas_call(
        table_kernel,
        out_shape=jax.ShapeDtypeStruct((3, GH * TAP, 2 * TAP), jnp.bfloat16),
        in_specs=[FULL],
        out_specs=FULL,
        compiler_params=pltpu.CompilerParams(vmem_limit_bytes=LIMIT),
        name="tables",
    )(first_row)


def slot_of(at, k):
    return lax.rem(at[1] - at[0] - k + 16, 4)


def filter_kernel(at, table, p0, p1, p2, p3, up, down, q_out, kv_out):
    pieces = (p0, p1, p2, p3)
    r = at[0]
    lane_group = lax.broadcasted_iota(jnp.int32, (TAP, HD), 1) // GW
    slots = [slot_of(at, k) for k in range(4)]
    for s in range(3):
        out = q_out.at[0] if s == 0 else kv_out.at[s - 1]
        tiles = []
        for k, slot in enumerate(slots):
            ahead = at[1] - r + 16
            from_up = lax.rem(ahead + 1 - lax.rem(ahead + 1, 2) - slot, 4) // 2
            from_down = lax.rem(ahead - 2 + lax.rem(ahead - 1, 2) - slot, 4) // 2
            own = jnp.logical_or(
                jnp.logical_and(slot == 2, r == 0),
                jnp.logical_and(lax.rem(slot, 2) == 1, r == 7),
            )
            before = jnp.where(
                own,
                pieces[(k + 1) % 4][s, TOK - TAP :, :],
                jnp.where(lax.rem(slot, 2) == 0, up[from_up, s], down[from_down, s]),
            )
            for t in range(TOK // TAP):
                now = pieces[k][s, t * TAP : (t + 1) * TAP, :]
                start = pl.multiple_of(slot * TOK + t * TAP, TAP)
                tiles.append((start, jnp.concatenate([before, now], axis=0)))
                before = now
        for i in range(0, len(tiles), 2):
            pair = jnp.concatenate([tiles[i][1], tiles[i + 1][1]], axis=1)
            wide = jnp.dot(table[s], pair, preferred_element_type=jnp.float32)
            for h in range(2):
                cols = slice(h * HD, (h + 1) * HD)
                res = wide[0:TAP, cols]
                for g in range(1, GH):
                    res = jnp.where(lane_group == g, wide[g * TAP : (g + 1) * TAP, cols], res)
                out[pl.ds(tiles[i + h][0], TAP), :] = res.astype(jnp.bfloat16)


def filter_pieces(at, table, pieces, up, down):
    return pl.pallas_call(
        filter_kernel,
        out_shape=[
            jax.ShapeDtypeStruct((1, ROWS, HD), jnp.bfloat16),
            jax.ShapeDtypeStruct((2, ROWS, HD), jnp.bfloat16),
        ],
        in_specs=[pl.BlockSpec(memory_space=pltpu.SMEM)] + [FULL] * 7,
        out_specs=[FULL] * 2,
        compiler_params=pltpu.CompilerParams(vmem_limit_bytes=LIMIT),
        name="filter",
    )(at, table, *pieces, up, down)


def attend_unit(scores, v, state, slot, diag, first):
    acc, top, total = state
    rows = slice(slot * TOK, (slot + 1) * TOK)
    cols = [
        piece[:, j * 128 : (j + 1) * 128] for piece in scores for j in range(piece.shape[1] // 128)
    ]
    if diag:
        row = lax.broadcasted_iota(jnp.int32, (TOK, 128), 0)
        col = lax.broadcasted_iota(jnp.int32, (TOK, 128), 1)
        for d in range(TOK // 128):
            j = len(cols) - TOK // 128 + d
            cols[j] = jnp.where(col + d * 128 <= row, cols[j], -1e30)
    high = functools.reduce(jnp.maximum, cols)
    high = jnp.broadcast_to(jnp.max(high, axis=1, keepdims=True), (TOK, 128))
    if not first:
        old = top[rows, :]
        high = jnp.maximum(old, high)
        fade = jnp.exp2((old - high) * EXP2_SCALE)
    weights = [jnp.exp2((s - high) * EXP2_SCALE) for s in cols]
    rounded = jnp.concatenate([w.astype(jnp.bfloat16) for w in weights], axis=1)
    added = functools.reduce(jnp.add, weights)
    res = None
    done = 0
    for values in v:
        size = values.shape[0]
        part = jnp.dot(
            rounded[:, done : done + size], values[...], preferred_element_type=jnp.float32
        )
        res = part if res is None else res + part
        done += size
    top[rows, :] = high
    if first:
        total[rows, :] = added
        acc[rows, :] = res
    else:
        total[rows, :] = total[rows, :] * fade + added
        acc[rows, :] = acc[rows, :] * fade + res


def attend_units(q, chunks, state, lengths, diag=False, first=False):
    units = []
    for slot, length in enumerate(lengths):
        used = []
        for parts in chunks:
            left = length
            for ref in parts:
                size = min(left, ref.shape[1])
                if size > 0:
                    used.append((ref.at[0, 0:size, :], ref.at[1, 0:size, :]))
                left -= size
        if used:
            units.append((slot, used))

    def scores_of(unit):
        slot, used = unit
        rows = q[slot * TOK : (slot + 1) * TOK, :]
        return [dot_nt(rows, k[...]) for k, _ in used]

    scores = scores_of(units[0])
    for i, (slot, used) in enumerate(units):
        following = scores_of(units[i + 1]) if i + 1 < len(units) else None
        attend_unit(scores, [v for _, v in used], state, slot, diag, first)
        scores = following


def attend_chunks(q, chunks, state, earlier):
    @pl.when(earlier)
    def _():
        attend_units(q, chunks, state, (TOK, TOK, 3 * TOK, 3 * TOK))

    @pl.when(jnp.logical_not(earlier))
    def _():
        attend_units(q, chunks, state, (0, 2 * TOK, 2 * TOK, 4 * TOK))


def begin_kernel(at, q, own, partner, acc, top, total):
    state = (acc, top, total)
    q = q.at[0]
    attend_units(q, [[own]], state, [(slot + 1) * TOK for slot in range(4)], diag=True, first=True)
    attend_chunks(q, [[partner]], state, lax.rem(at[0], 2) == 1)


def near_kernel(at, q, below, above, below_2, above_2, acc_in, top_in, total_in, acc, top, total):
    state = (acc, top, total)
    take((acc_in, top_in, total_in), state)
    q = q.at[0]
    y = at[0] // 2
    attend_chunks(q, [[below], [below_2]], state, y > 0)
    attend_chunks(q, [[above], [above_2]], state, y == 3)


def take(state_in, state):
    for src, dst in zip(state_in, state):
        dst[...] = src[...]


def far_kernel(at, q, fa, fb, acc_in, top_in, total_in, acc, top, total):
    state = (acc, top, total)
    take((acc_in, top_in, total_in), state)
    attend_chunks(q.at[0], [[fa, fb]], state, at[0] >= 4)


def end_kernel(at, q, fa, fb, acc_in, top_in, total_in, o0, o1, o2, o3, acc, top, total):
    state = (acc, top, total)
    take((acc_in, top_in, total_in), state)
    attend_chunks(q.at[0], [[fa, fb]], state, at[0] >= 4)
    for k, out in enumerate((o0, o1, o2, o3)):
        rows = pl.ds(pl.multiple_of(slot_of(at, k) * TOK, TAP), TOK)
        whole = jnp.sum(total[rows, :], axis=1, keepdims=True)
        out[...] = (acc[rows, :] / whole).astype(jnp.bfloat16)


STATE = [jax.ShapeDtypeStruct((ROWS, HD), jnp.float32)] * 3
UNIT_FLOPS = 4 * TOK * TOK * HD


def attend_call(kernel, name, units, outs, scratch, args):
    return pl.pallas_call(
        kernel,
        out_shape=outs,
        in_specs=[pl.BlockSpec(memory_space=pltpu.SMEM)] + [FULL] * (len(args) - 1),
        out_specs=[FULL] * len(outs),
        scratch_shapes=scratch,
        compiler_params=pltpu.CompilerParams(vmem_limit_bytes=LIMIT),
        cost_estimate=pl.CostEstimate(
            flops=2 * units * UNIT_FLOPS,
            bytes_accessed=6 * 2**20,
            transcendentals=units * TOK * TOK,
        ),
        name=name,
    )(*args)


def squares_kernel(p0, p1, p2, p3, out):
    wide = sum(jnp.square(p[...].astype(jnp.float32)) for p in (p0, p1, p2, p3))
    out[...] = jnp.sum(wide.T, axis=0, keepdims=True)


def norm_kernel(at, p0, p1, p2, p3, s0, s1, s2, s3, gain, out):
    power = (s0[...] + s1[...] + s2[...] + s3[...]) * (1.0 / CH)
    scale = jnp.broadcast_to(lax.rsqrt(power + 1e-6), (HD, TOK)).T
    for k, piece in enumerate((p0, p1, p2, p3)):
        cols = pl.ds(pl.multiple_of(lax.rem(at[2] + k, 4) * HD, HD), HD)
        out[:, cols] = (piece[...].astype(jnp.float32) * gain[:, cols] * scale).astype(jnp.bfloat16)


def local(streams, filters, gain):
    y, z, c = lax.axis_index("y"), lax.axis_index("z"), lax.axis_index("c")
    r = jnp.where(lax.rem(y, 2) == 0, z, 7 - z)
    at = jnp.stack([2 * y + c, z, y + r]).astype(jnp.int32)

    pieces = []
    for k in range(4):
        col = lax.rem(y + r + k, 4) * HD
        piece = lax.dynamic_slice(streams, (0, 0, col), (3, TOK, HD))
        pieces.append(send(piece, to_owner(k)))

    mine = lax.dynamic_slice(filters, (0, lax.rem(z, 4) * GH, 0), (3, GH, TAP))
    other = send(mine, swap_core)
    taps = jnp.where(c == z // 4, mine, other).reshape(3 * GH, TAP).astype(jnp.float32)
    table = make_tables(jnp.pad(taps[:, ::-1], ((0, 0), (1, TAP - 1))))
    t0, t1, t2, t3 = (p[:, TOK - TAP :, :] for p in pieces)
    same = lax.rem(z + c, 2) == 0
    up = send(jnp.where(same, jnp.stack([t0, t2]), jnp.stack([t1, t3])), shift_owner(1))
    down = send(jnp.where(same, jnp.stack([t1, t3]), jnp.stack([t0, t2])), shift_owner(-1))
    queries, own = filter_pieces(at, table, pieces, up, down)

    from_below = send(own, shift_y(1))
    from_above = send(own, shift_y(-1))
    partner = send(own, swap_core)
    state = attend_call(
        begin_kernel, "attend_begin", 18, STATE, [], (at, queries, own, partner)
    )
    half = ROWS // 2
    from_below, from_above, state = lax.optimization_barrier((from_below, from_above, state))
    far_a = send(from_below[:, :half], shift_y(1))
    far_b = send(from_above[:, half:], shift_y(-1))
    swapped_below = send(from_below, swap_core)
    swapped_above = send(from_above, swap_core)
    state = attend_call(
        near_kernel,
        "attend_near",
        32,
        STATE,
        [],
        (at, queries, from_below, from_above, swapped_below, swapped_above, *state),
    )
    far_a, far_b, state = lax.optimization_barrier((far_a, far_b, state))
    swapped_a = send(far_a, swap_core)
    swapped_b = send(far_b, swap_core)
    state = attend_call(far_kernel, "attend_far", 8, STATE, [], (at, queries, far_a, far_b, *state))
    pieces = attend_call(
        end_kernel,
        "attend_end",
        8,
        [jax.ShapeDtypeStruct((TOK, HD), jnp.bfloat16)] * 4,
        [pltpu.VMEM((ROWS, HD), jnp.float32)] * 3,
        (at, queries, swapped_a, swapped_b, *state),
    )

    home = [send_home(p, k) for k, p in enumerate(pieces)]
    part = pl.pallas_call(
        squares_kernel,
        out_shape=jax.ShapeDtypeStruct((1, TOK), jnp.float32),
        in_specs=[FULL] * 4,
        out_specs=FULL,
        name="squares",
    )(*home)
    part = part + send(part, swap_core)
    sums = [part] + [send(part, shift_x(i)) for i in (1, 2, 3)]
    return pl.pallas_call(
        norm_kernel,
        out_shape=jax.ShapeDtypeStruct((TOK, 4 * HD), jnp.bfloat16),
        in_specs=[pl.BlockSpec(memory_space=pltpu.SMEM)] + [FULL] * 9,
        out_specs=FULL,
        name="norm",
    )(at, *home, *sums, gain.reshape(1, 4 * HD))


def solution(mesh):
    split = Mesh(mesh.devices.reshape(NY, NZ, NX, NC), AXES)
    ctx, grp = ("y", "z"), ("x", "c")
    return jax.shard_map(
        local,
        mesh=split,
        in_specs=(P(None, ctx, grp), P(None, grp, None), P(grp)),
        out_specs=P(ctx, grp),
        check_vma=False,
    )
```
